32 devices in a mesh: groups: 2 (over y), fsdp: 4 (over x, core), tensor: 4 (over z).
Axes of the slice: x: 2, y: 2, z: 4, core: 2. Of those that a mesh axis runs over, the one named last changes fastest.
Arguments:
- video: bfloat16 [8, 256, 3072], P(('groups', 'fsdp'), 'tensor'), parts along dimension 0, may hold values from -6 to 6
- timesteps: int32 [8, 3], P(('groups', 'fsdp')), parts along dimension 0, may hold values from 1 to 999
- text_keys: bfloat16 [8, 256, 512], P(('groups', 'fsdp'), None, 'tensor'), parts along dimension 0, may hold values from -490 to 490
- text_values: bfloat16 [8, 256, 512], P(('groups', 'fsdp'), None, 'tensor'), parts along dimension 0, may hold values from -6 to 6
- text_lengths: int32 [8], P(('groups', 'fsdp')), parts along dimension 0, may hold values from 64 to 256, as said below
- base_weights: bfloat16 [4, 3072, 512], P(None, None, 'tensor'), may hold values from -0.109375 to 0.109375
- delta_values: bfloat16 [4, 3072, 512], P(None, ('fsdp', 'tensor')), may hold values from -6 to 6
- delta_scales: float32 [4, 24, 4], replicated, may hold values from 0.002 to 0.02
- q_gain: float32 [128], replicated, may hold values from 1 to 2
- k_gain: float32 [128], replicated, may hold values from 1 to 2
- mod_weight: bfloat16 [256, 6, 3072], P(None, None, 'tensor'), may hold values from -0.75 to 0.75
- fc_in: bfloat16 [3072, 2560], P(None, 'tensor'), may hold values from -0.109375 to 0.109375
- fc_out: bfloat16 [2560, 3072], P('tensor'), may hold values from -0.125 to 0.125
Outputs:
- latent: bfloat16 [8, 256, 3072], P(('groups', 'fsdp'), 'tensor'), parts along dimension 0
- velocity: bfloat16 [8, 2, 256, 3072], P(('groups', 'fsdp'), None, 'tensor'), parts along dimension 0
The draws below stay inside these ranges and needn't reach their ends.
There are 2 independent parts, one for each index of `groups`. The reference program is written for one: setup_inputs(seed, part) draws one part's arguments, and reference() takes and returns one part's arrays. A program takes and returns all parts, laid end to end along the dimension named above; an argument that names none is the same for every part. Nothing has to cross between parts.
Inputs may be any that keep to these rules, and one draw needn't show every extreme that they name: `text_lengths`: each sample's number of valid text tokens.
All inputs are finite; a program needn't handle non-finite values.
Results may differ from the reference program's by a relative error of at most 0.038.
Values may be sent and summed in bfloat16 or wider, within the bound.
A program may use at most 64 MiB of HBM per device.

```python
import math
import jax
import jax.numpy as jnp
from jax import lax

D = 3072
HEAD_DIM = 128
FREQ = 256
HEAD_DEV = 1
FF_DEV = 640
TXT = 256
STEPS = 2
VID = 256
HEADS = 4
FFW = 2560
SAMPLES = 4
N_TENSOR = 4


def draw_text_keys(key, part):
    key = jax.random.fold_in(key, 11)
    subkeys = jax.random.split(key, 1)
    shape = (SAMPLES, TXT, HEADS * HEAD_DIM)
    values = jnp.clip(jax.random.normal(subkeys[0], shape, jnp.float32), -6.0, 6.0)
    return values.astype(jnp.bfloat16)


def draw_text_lengths(key, part):
    key = jax.random.fold_in(key, 23)
    subkeys = jax.random.split(key, 2)
    drawn = jax.random.randint(subkeys[0], (SAMPLES,), TXT // 4, TXT + 1)
    fullest = jax.random.randint(subkeys[1], (), 0, SAMPLES)
    return jnp.where(jnp.arange(SAMPLES) == fullest, TXT, drawn).astype(jnp.int32)


def set_ends(result, own_key, smallest, largest):
    shape = result.shape
    place = [jax.random.randint(jax.random.fold_in(own_key, axis), (), 0, shape[axis]) for axis in range(len(shape))]
    result = result.at[tuple(place)].set(smallest)
    longest = shape.index(max(shape))
    place[longest] = (place[longest] + 1) % shape[longest]
    return result.at[tuple(place)].set(largest)


def levels(rng, dims, shards, least, largest):
    loudness, own = 1.0, jax.random.fold_in(rng, 6)
    for dim, shards_of in shards:
        heights = jnp.exp(jax.random.uniform(jax.random.fold_in(own, dim), (shards_of,), jnp.float32, least / len(shards), largest / len(shards)))
        loudness = loudness * jnp.repeat(heights, dims[dim] // shards_of).reshape([-1 if axis == dim else 1 for axis in range(len(dims))])
    return loudness


def bell_draw(own_key, extent, deviation, most, shards=(), kind=jnp.bfloat16):
    array = jax.random.normal(own_key, extent, jnp.float32) * deviation
    if len(shards) > 0:
        array = levels(own_key, extent, shards, -0.22, 0.18) * array
    return jnp.clip(array, min=-most, max=most).astype(kind)


def setup_inputs(seed: int = 0, part: int = 0) -> dict:
    streams_of = jax.random.split(jax.random.key(seed), 14)
    part_splits = jax.random.split(jax.random.fold_in(streams_of[13], part), 14)
    return {
        "video": bell_draw(part_splits[0], (SAMPLES, VID, D), 1.0, 6.0, ((0, 4), (1, 4))),
        "timesteps": set_ends(jax.random.randint(part_splits[1], (SAMPLES, STEPS + 1), 1, 1000), jax.random.fold_in(part_splits[1], 1), 1, 999).astype(jnp.int32),
        "text_keys": draw_text_keys(jax.random.fold_in(jax.random.fold_in(streams_of[13], part), 71), part),
        "text_values": bell_draw(part_splits[3], (SAMPLES, TXT, HEADS * HEAD_DIM), 1.0, 6.0, ((0, 4), (2, 4))),
        "text_lengths": draw_text_lengths(jax.random.fold_in(jax.random.fold_in(streams_of[13], part), 71), part),
        "base_weights": bell_draw(streams_of[5], (4, D, HEADS * HEAD_DIM), D ** -0.5, 0.109375, ((2, 4),)),
        "delta_values": bell_draw(streams_of[6], (4, D, HEADS * HEAD_DIM), 1.0, 6.0, ((1, 16),)),
        "delta_scales": jnp.clip(jnp.exp(jax.random.uniform(streams_of[7], (4, D // HEAD_DIM, HEADS), jnp.float32, math.log(0.002), math.log(0.02))), 0.002, 0.02),
        "q_gain": jnp.clip(jnp.exp(jax.random.uniform(streams_of[8], (HEAD_DIM,), jnp.float32, math.log(1.0), math.log(2.0))), 1.0, 2.0),
        "k_gain": jnp.clip(jnp.exp(jax.random.uniform(streams_of[9], (HEAD_DIM,), jnp.float32, math.log(1.0), math.log(2.0))), 1.0, 2.0),
        "mod_weight": bell_draw(streams_of[10], (FREQ, 6, D), (FREQ // 4) ** -0.5, 0.75, ((2, 4),)),
        "fc_in": bell_draw(streams_of[11], (D, FFW), D ** -0.5, 0.109375, ((1, 4),)),
        "fc_out": bell_draw(streams_of[12], (FFW, D), FFW ** -0.5, 0.125, ((0, 4),)),
    }


def layer_norm(values):
    center = values - lax.optimization_barrier(jnp.mean(values, axis=-1, keepdims=True))
    spread = lax.optimization_barrier(jnp.mean(center * center, axis=-1, keepdims=True))
    return center * lax.rsqrt(spread + 1e-06)

def rms_scale(values, gain):
    power = lax.optimization_barrier(jnp.mean(values * values, axis=-1, keepdims=True))
    return values * lax.rsqrt(power + 1e-06) * gain

def time_embed(times):
    half_count = FREQ // 2
    ladder = jnp.exp(-math.log(10000.0) * jnp.arange(half_count, dtype=jnp.float32) / half_count)
    angles = times.astype(jnp.float32)[:, None] * ladder[None, :]
    return jnp.concatenate([jnp.cos(angles), jnp.sin(angles)], axis=1)

def reference(video, timesteps, text_keys, text_values, text_lengths, base_weights, delta_values, delta_scales, q_gain, k_gain, mod_weight, fc_in, fc_out):
    head_width = HEAD_DEV * HEAD_DIM
    scale_full = jnp.repeat(jnp.repeat(delta_scales, HEAD_DIM, axis=1), HEAD_DIM, axis=2)
    weights = (base_weights.astype(jnp.float32) + delta_values.astype(jnp.float32) * scale_full).astype(jnp.bfloat16)
    out_groups = weights[3].reshape(D, N_TENSOR, head_width).astype(jnp.float32)
    down_groups = fc_out.reshape(N_TENSOR, FF_DEV, D).astype(jnp.float32)

    def one_sample(items):
        frames, times, text_k, text_v, text_len = items
        embedding = jax.nn.silu(time_embed(times[:STEPS])).astype(jnp.bfloat16)
        modulation = jnp.einsum('sf,fkd->skd', embedding.astype(jnp.float32), mod_weight.astype(jnp.float32))
        latent = frames.astype(jnp.float32)
        text_valid = jnp.arange(TXT) < text_len
        key_valid = jnp.concatenate([jnp.ones((VID,), dtype=bool), text_valid])
        velocities = []
        for step in range(STEPS):
            mods = modulation[step]
            attn_in = (layer_norm(latent) * (1.0 + mods[1]) + mods[0]).astype(jnp.bfloat16)
            query = jnp.dot(attn_in, weights[0], preferred_element_type=jnp.float32).reshape(VID, HEADS, HEAD_DIM)
            key_part = jnp.dot(attn_in, weights[1], preferred_element_type=jnp.float32).reshape(VID, HEADS, HEAD_DIM)
            value_part = jnp.dot(attn_in, weights[2], preferred_element_type=jnp.float32).astype(jnp.bfloat16).reshape(VID, HEADS, HEAD_DIM)
            query = rms_scale(query, q_gain).astype(jnp.bfloat16)
            key_part = rms_scale(key_part, k_gain).astype(jnp.bfloat16)
            all_keys = jnp.concatenate([key_part, text_k.reshape(TXT, HEADS, HEAD_DIM)], axis=0)
            all_values = jnp.concatenate([value_part, text_v.reshape(TXT, HEADS, HEAD_DIM)], axis=0)
            scores = jnp.einsum('qhd,khd->hqk', query.astype(jnp.float32), all_keys.astype(jnp.float32)) / math.sqrt(HEAD_DIM)
            scores = jnp.where(key_valid[None, None, :], scores, -jnp.inf)
            soft = jax.nn.softmax(scores, axis=-1).astype(jnp.bfloat16)
            mixed = jnp.einsum('hqk,khd->qhd', soft.astype(jnp.float32), all_values.astype(jnp.float32)).astype(jnp.bfloat16)
            mixed = mixed.reshape(VID, N_TENSOR, head_width).astype(jnp.float32)
            terms = jnp.einsum('qgc,dgc->gqd', mixed, out_groups).astype(jnp.bfloat16)
            terms = lax.optimization_barrier(terms)
            attn = lax.optimization_barrier(jnp.sum(terms.astype(jnp.float32), axis=0))
            midway = latent + mods[2] * attn
            mlp_in = (layer_norm(midway) * (1.0 + mods[4]) + mods[3]).astype(jnp.bfloat16)
            hidden = jax.nn.gelu(jnp.dot(mlp_in, fc_in, preferred_element_type=jnp.float32), approximate=True).astype(jnp.bfloat16)
            hidden = hidden.reshape(VID, N_TENSOR, FF_DEV).astype(jnp.float32)
            down_terms = jnp.einsum('qgc,gcd->gqd', hidden, down_groups).astype(jnp.bfloat16)
            down_terms = lax.optimization_barrier(down_terms)
            mlp = lax.optimization_barrier(jnp.sum(down_terms.astype(jnp.float32), axis=0))
            update = mods[2] * attn + mods[5] * mlp
            velocities.append(update.astype(jnp.bfloat16))
            step_size = (times[step + 1] - times[step]).astype(jnp.float32) / 1000.0
            latent = latent + step_size * update
        return (latent.astype(jnp.bfloat16), jnp.stack(velocities))
    return lax.map(one_sample, (video, timesteps, text_keys, text_values, text_lengths))
```

```python
import functools
import math

import jax
import jax.numpy as jnp
from jax import lax
from jax.experimental import pallas as pl
from jax.experimental.pallas import tpu as pltpu
from jax.sharding import PartitionSpec as P

STEPS = 2


def layer_norm(values):
    center = values - jnp.mean(values, axis=-1, keepdims=True)
    spread = jnp.mean(center * center, axis=-1, keepdims=True)
    return center * lax.rsqrt(spread + 1e-06)


def rms_scale(values, gain):
    power = jnp.mean(values * values, axis=-1, keepdims=True)
    return values * lax.rsqrt(power + 1e-06) * gain


def time_embed(times, freq_count):
    half_count = freq_count // 2
    ladder = jnp.exp(-math.log(10000.0) * jnp.arange(half_count, dtype=jnp.float32) / half_count)
    angles = times.astype(jnp.float32)[:, None] * ladder[None, :]
    return jnp.concatenate([jnp.cos(angles), jnp.sin(angles)], axis=1)


def line_copy(src, dst, send_sem, recv_sem, target):
    return pltpu.make_async_remote_copy(
        src_ref=src,
        dst_ref=dst,
        send_sem=send_sem,
        recv_sem=recv_sem,
        device_id={"tensor": target},
        device_id_type=pl.DeviceIdType.MESH,
    )


def greet_neighbours(z, n):
    barrier = pltpu.get_barrier_semaphore()

    @pl.when(z > 0)
    def _():
        pl.semaphore_signal(
            barrier, inc=1, device_id={"tensor": z - 1}, device_id_type=pl.DeviceIdType.MESH
        )

    @pl.when(z < n - 1)
    def _():
        pl.semaphore_signal(
            barrier, inc=1, device_id={"tensor": z + 1}, device_id_type=pl.DeviceIdType.MESH
        )

    pl.semaphore_wait(barrier, jnp.where(z > 0, 1, 0) + jnp.where(z < n - 1, 1, 0))


class Gather:
    def __init__(self, z, n, buf, send_sem, recv_sem):
        self.z, self.n, self.buf, self.send_sem, self.recv_sem = z, n, buf, send_sem, recv_sem

    def copy(self, c, owner, way):
        block = self.buf.at[c, owner]
        target = self.z + 1 if way == 0 else self.z - 1
        return line_copy(
            block, block, self.send_sem.at[way, c, owner], self.recv_sem.at[c, owner], target
        )

    def start(self, c):
        z, n = self.z, self.n

        @pl.when(z < n - 1)
        def _():
            self.copy(c, z, 0).start()

        @pl.when(z > 0)
        def _():
            self.copy(c, z, 1).start()

    def forward(self, c):
        z, n = self.z, self.n
        for d in range(1, n):

            @pl.when(z - d >= 0)
            def _():
                self.copy(c, z - d, 0).wait_recv()

                @pl.when(z < n - 1)
                def _():
                    self.copy(c, z - d, 0).start()

            @pl.when(z + d <= n - 1)
            def _():
                self.copy(c, z + d, 1).wait_recv()

                @pl.when(z > 0)
                def _():
                    self.copy(c, z + d, 1).start()

    def finish(self, c):
        z, n = self.z, self.n
        for o in range(n):

            @pl.when((z >= o) & (z < n - 1))
            def _():
                self.copy(c, o, 0).wait_send()

            @pl.when((z <= o) & (z > 0))
            def _():
                self.copy(c, o, 1).wait_send()


class Scatter:
    def __init__(self, z, n, term, recv, send_sem, recv_sem):
        self.z, self.n, self.term, self.recv = z, n, term, recv
        self.send_sem, self.recv_sem = send_sem, recv_sem

    def copy(self, c, o, way):
        target = self.z + 1 if way == 0 else self.z - 1
        return line_copy(
            self.term.at[c, o],
            self.recv.at[way, c, o],
            self.send_sem.at[c, o],
            self.recv_sem.at[way, c, o],
            target,
        )

    def ends(self, c):
        z, n = self.z, self.n
        for k in range(n - 1):

            @pl.when(z == 0)
            def _():
                self.copy(c, n - 1 - k, 0).start()

            @pl.when(z == n - 1)
            def _():
                self.copy(c, k, 1).start()

    def add(self, c, o, way):
        self.copy(c, o, way).wait_recv()
        total = self.term[c, o].astype(jnp.float32) + self.recv[way, c, o].astype(jnp.float32)
        self.term[c, o] = total.astype(jnp.bfloat16)
        self.copy(c, o, way).start()

    def forward(self, c):
        z, n = self.z, self.n
        for k in range(n - 1):
            right, left = n - 1 - k, k

            @pl.when((z > 0) & (z < right))
            def _():
                self.add(c, right, 0)

            @pl.when((z < n - 1) & (z > left))
            def _():
                self.add(c, left, 1)

    def collect(self, c, total):
        z, n = self.z, self.n
        total[...] = self.term[c, z].astype(jnp.float32)

        @pl.when(z > 0)
        def _():
            self.copy(c, z, 0).wait_recv()
            total[...] += self.recv[0, c, z].astype(jnp.float32)

        @pl.when(z < n - 1)
        def _():
            self.copy(c, z, 1).wait_recv()
            total[...] += self.recv[1, c, z].astype(jnp.float32)

    def finish(self, c):
        z, n = self.z, self.n
        for o in range(n):

            @pl.when(z < o)
            def _():
                self.copy(c, o, 0).wait_send()

            @pl.when(z > o)
            def _():
                self.copy(c, o, 1).wait_send()


def tail_kernel(
    n,
    chunks,
    last,
    step_ref,
    mixed_ref,
    out_weight_ref,
    latent_ref,
    mods_ref,
    next_ref,
    fc_in_ref,
    fc_out_ref,
    new_ref,
    velocity_ref,
    gathered_ref,
    attn_term,
    attn_recv,
    mlp_in_all,
    mlp_term,
    mlp_recv,
    attn_sum,
    total,
    hidden_ref,
    as_send,
    as_recv,
    mg_send,
    mg_recv,
    ms_send,
    ms_recv,
    ag_send,
    ag_recv,
):
    z = lax.axis_index("tensor")
    tokens, width = latent_ref.shape
    rows = tokens // chunks
    tile = math.gcd(width, 768)
    attn_out = Scatter(z, n, attn_term, attn_recv, as_send, as_recv)
    mlp_gather = Gather(z, n, mlp_in_all, mg_send, mg_recv)
    mlp_out = Scatter(z, n, mlp_term, mlp_recv, ms_send, ms_recv)
    next_gather = None if last else Gather(z, n, gathered_ref, ag_send, ag_recv)

    greet_neighbours(z, n)
    for c in range(chunks):
        part = mixed_ref[c * n * rows : (c + 1) * n * rows, :]
        for t in range(0, width, tile):
            product = lax.dot_general(
                part,
                out_weight_ref[t : t + tile, :],
                (((1,), (1,)), ((), ())),
                preferred_element_type=jnp.float32,
            ).astype(jnp.bfloat16)
            attn_term[c, :, :, t : t + tile] = product.reshape(n, rows, tile)
        attn_out.ends(c)

    def after_attention(c):
        attn_out.forward(c)
        attn_out.collect(c, attn_sum.at[c])
        own = slice(c * rows, (c + 1) * rows)
        gated = mods_ref[2:3, :] * attn_sum[c]
        midway = latent_ref[own, :] + gated
        attn_sum[c] = gated
        mlp_in = layer_norm(midway) * (1.0 + mods_ref[4:5, :]) + mods_ref[3:4, :]
        mlp_in_all[c, z] = mlp_in.astype(jnp.bfloat16)
        mlp_gather.start(c)

    def feed_forward(c):
        mlp_gather.forward(c)
        tokens_in = mlp_in_all[c].reshape(n * rows, width)
        hidden = jax.nn.gelu(
            jnp.dot(tokens_in, fc_in_ref[...], preferred_element_type=jnp.float32),
            approximate=True,
        )
        hidden_ref[...] = hidden.astype(jnp.bfloat16)
        for t in range(0, width, tile):
            product = jnp.dot(
                hidden_ref[...], fc_out_ref[:, t : t + tile], preferred_element_type=jnp.float32
            ).astype(jnp.bfloat16)
            mlp_term[c, :, :, t : t + tile] = product.reshape(n, rows, tile)
        mlp_out.ends(c)

    def after_feed_forward(c):
        mlp_out.forward(c)
        mlp_out.collect(c, total)
        own = slice(c * rows, (c + 1) * rows)
        update = attn_sum[c] + mods_ref[5:6, :] * total[...]
        velocity_ref[own, :] = update.astype(jnp.bfloat16)
        fresh = latent_ref[own, :] + step_ref[0:1, 0:1] * update
        new_ref[own, :] = fresh.astype(new_ref.dtype)
        if not last:
            attn_in = layer_norm(fresh) * (1.0 + next_ref[1:2, :]) + next_ref[0:1, :]
            gathered_ref[c, z] = attn_in.astype(jnp.bfloat16)
            next_gather.start(c)

    stages = [after_attention, feed_forward, after_feed_forward]
    if not last:
        stages.append(lambda c: next_gather.forward(c))
    for tick in range(chunks + len(stages) - 1):
        for place, stage in enumerate(stages):
            if 0 <= tick - place < chunks:
                stage(tick - place)
    for c in range(chunks):
        attn_out.finish(c)
        mlp_gather.finish(c)
        mlp_out.finish(c)
        if not last:
            next_gather.finish(c)


def chunk_count(tokens):
    return max(1, min(2, tokens // 16))


def block_tail(n, last, step_size, mixed, out_weight, latent, mods, next_mods, fc_in, fc_out):
    tokens, width = latent.shape
    chunks = chunk_count(tokens)
    rows = tokens // chunks
    blocks = (chunks, n, rows, width)
    vmem = pl.BlockSpec(memory_space=pltpu.VMEM)
    gathered_shape = (8, 128) if last else blocks
    dma = pltpu.SemaphoreType.DMA
    return pl.pallas_call(
        functools.partial(tail_kernel, n, chunks, last),
        out_shape=(
            jax.ShapeDtypeStruct((tokens, width), jnp.bfloat16 if last else jnp.float32),
            jax.ShapeDtypeStruct((tokens, width), jnp.bfloat16),
            jax.ShapeDtypeStruct(gathered_shape, jnp.bfloat16),
        ),
        in_specs=[vmem] * 8,
        out_specs=(vmem, vmem, vmem),
        scratch_shapes=[
            pltpu.VMEM(blocks, jnp.bfloat16),
            pltpu.VMEM((2,) + blocks, jnp.bfloat16),
            pltpu.VMEM(blocks, jnp.bfloat16),
            pltpu.VMEM(blocks, jnp.bfloat16),
            pltpu.VMEM((2,) + blocks, jnp.bfloat16),
            pltpu.VMEM((chunks, rows, width), jnp.float32),
            pltpu.VMEM((rows, width), jnp.float32),
            pltpu.VMEM((n * rows, fc_in.shape[1]), jnp.bfloat16),
            dma((chunks, n)),
            dma((2, chunks, n)),
            dma((2, chunks, n)),
            dma((chunks, n)),
            dma((chunks, n)),
            dma((2, chunks, n)),
            dma((2, chunks, n)),
            dma((chunks, n)),
        ],
        compiler_params=pltpu.CompilerParams(
            collective_id=1 if last else 0,
            has_side_effects=True,
            vmem_limit_bytes=48 * 1024 * 1024,
        ),
        cost_estimate=pl.CostEstimate(
            flops=4 * n * tokens * width * fc_in.shape[1],
            bytes_accessed=4 * width * fc_in.shape[1],
            transcendentals=n * tokens * fc_in.shape[1],
        ),
    )(step_size, mixed, out_weight, latent, mods, next_mods, fc_in, fc_out)


def shards(
    video,
    timesteps,
    text_keys,
    text_values,
    text_lengths,
    base_weights,
    delta_values,
    delta_scales,
    q_gain,
    k_gain,
    mod_weight,
    fc_in,
    fc_out,
):
    head_dim = q_gain.shape[0]
    head_width = base_weights.shape[2]
    heads_here = head_width // head_dim
    text_count = text_keys.shape[1]
    column_index = lax.axis_index("tensor")
    embedding = jax.nn.silu(time_embed(timesteps[0, :STEPS], mod_weight.shape[0])).astype(
        jnp.bfloat16
    )
    mod_part = jnp.einsum("sf,fkd->skd", embedding, mod_weight, preferred_element_type=jnp.float32)
    modulation = lax.all_gather(mod_part, "tensor", axis=2, tiled=True)
    own_delta = lax.all_to_all(delta_values, "tensor", split_axis=2, concat_axis=1, tiled=True)
    own_scales = lax.dynamic_slice_in_dim(delta_scales, column_index * heads_here, heads_here, 2)
    row_scales = jnp.repeat(own_scales, head_dim, axis=1)
    dequantize_piece = lax.all_gather(own_delta, "fsdp", axis=1, tiled=True)
    scale_full = jnp.repeat(row_scales, head_dim, axis=2)
    weights = (
        base_weights.astype(jnp.float32) + dequantize_piece.astype(jnp.float32) * scale_full
    ).astype(jnp.bfloat16)
    qkv_weights = weights[:3]
    out_weight = weights[3]
    latent = video[0].astype(jnp.float32)
    text_valid = jnp.arange(text_count) < text_lengths[0]
    text_k = text_keys[0]
    text_v = text_values[0]
    velocities = []
    n = lax.axis_size("tensor")
    width = latent.shape[1]
    chunks = chunk_count(latent.shape[0])
    first = modulation[0]
    attn_in = (layer_norm(latent) * (1.0 + first[1]) + first[0]).astype(jnp.bfloat16)
    piece = lax.all_gather(attn_in, "tensor", axis=0, tiled=True)
    piece = piece.reshape(n, chunks, -1, width).swapaxes(0, 1).reshape(-1, width)
    for step in range(STEPS):
        mods = modulation[step]
        count = piece.shape[0]
        joined = jnp.einsum("rd,kdc->rkc", piece, qkv_weights, preferred_element_type=jnp.float32)
        query = rms_scale(joined[:, 0].reshape(count, heads_here, head_dim), q_gain).reshape(
            count, head_width
        )
        key_part = rms_scale(joined[:, 1].reshape(count, heads_here, head_dim), k_gain).reshape(
            count, head_width
        )
        projected = jnp.stack([query, key_part, joined[:, 2]], axis=1).astype(jnp.bfloat16)
        video_count = projected.shape[0]
        query = projected[:, 0].reshape(video_count, heads_here, head_dim)
        all_keys = jnp.concatenate([projected[:, 1], text_k], axis=0).reshape(
            -1, heads_here, head_dim
        )
        all_values = jnp.concatenate([projected[:, 2], text_v], axis=0).reshape(
            -1, heads_here, head_dim
        )
        key_valid = jnp.concatenate([jnp.ones((video_count,), dtype=bool), text_valid])
        scores = jnp.einsum(
            "qhd,khd->hqk", query, all_keys, preferred_element_type=jnp.float32
        ) / math.sqrt(head_dim)
        scores = jnp.where(key_valid[None, None, :], scores, -jnp.inf)
        soft = jax.nn.softmax(scores, axis=-1).astype(jnp.bfloat16)
        mixed = jnp.einsum(
            "hqk,khd->qhd", soft, all_values, preferred_element_type=jnp.float32
        ).astype(jnp.bfloat16)
        mixed = mixed.reshape(video_count, head_width)
        step_size = (timesteps[0, step + 1] - timesteps[0, step]).astype(jnp.float32) / 1000.0
        last = step == STEPS - 1
        latent, velocity, gathered = block_tail(
            n,
            last,
            step_size.reshape(1, 1),
            mixed,
            out_weight,
            latent,
            mods,
            mods if last else modulation[step + 1],
            fc_in,
            fc_out,
        )
        velocities.append(velocity)
        if not last:
            piece = gathered.reshape(-1, width)
    return (latent[None], jnp.stack(velocities)[None])


def solution(mesh):
    in_specs = (
        P(("groups", "fsdp"), "tensor", None),
        P(("groups", "fsdp"), None),
        P(("groups", "fsdp"), None, "tensor"),
        P(("groups", "fsdp"), None, "tensor"),
        P(("groups", "fsdp")),
        P(None, None, "tensor"),
        P(None, ("fsdp", "tensor"), None),
        P(),
        P(),
        P(),
        P(None, None, "tensor"),
        P(None, "tensor"),
        P("tensor", None),
    )
    out_specs = (P(("groups", "fsdp"), "tensor", None), P(("groups", "fsdp"), None, "tensor", None))
    return jax.shard_map(shards, mesh=mesh, in_specs=in_specs, out_specs=out_specs, check_vma=False)
```

```python
import functools
import math

import jax
import jax.numpy as jnp
from jax import lax
from jax.experimental import pallas as pl
from jax.experimental.pallas import tpu as pltpu
from jax.sharding import PartitionSpec as P

STEPS = 2


def layer_norm(values):
    center = values - jnp.mean(values, axis=-1, keepdims=True)
    spread = jnp.mean(center * center, axis=-1, keepdims=True)
    return center * lax.rsqrt(spread + 1e-06)


def rms_scale(values, gain):
    power = jnp.mean(values * values, axis=-1, keepdims=True)
    return values * lax.rsqrt(power + 1e-06) * gain


def time_embed(times, freq_count):
    half_count = freq_count // 2
    ladder = jnp.exp(-math.log(10000.0) * jnp.arange(half_count, dtype=jnp.float32) / half_count)
    angles = times.astype(jnp.float32)[:, None] * ladder[None, :]
    return jnp.concatenate([jnp.cos(angles), jnp.sin(angles)], axis=1)


def line_copy(src, dst, send_sem, recv_sem, target):
    return pltpu.make_async_remote_copy(
        src_ref=src,
        dst_ref=dst,
        send_sem=send_sem,
        recv_sem=recv_sem,
        device_id={"tensor": target},
        device_id_type=pl.DeviceIdType.MESH,
    )


def greet_neighbours(z, n):
    barrier = pltpu.get_barrier_semaphore()

    @pl.when(z > 0)
    def _():
        pl.semaphore_signal(
            barrier, inc=1, device_id={"tensor": z - 1}, device_id_type=pl.DeviceIdType.MESH
        )

    @pl.when(z < n - 1)
    def _():
        pl.semaphore_signal(
            barrier, inc=1, device_id={"tensor": z + 1}, device_id_type=pl.DeviceIdType.MESH
        )

    pl.semaphore_wait(barrier, jnp.where(z > 0, 1, 0) + jnp.where(z < n - 1, 1, 0))


class Gather:
    def __init__(self, z, n, buf, send_sem, recv_sem):
        self.z, self.n, self.buf, self.send_sem, self.recv_sem = z, n, buf, send_sem, recv_sem

    def copy(self, c, owner, way):
        block = self.buf.at[c, owner]
        target = self.z + 1 if way == 0 else self.z - 1
        return line_copy(
            block, block, self.send_sem.at[way, c, owner], self.recv_sem.at[c, owner], target
        )

    def start(self, c):
        z, n = self.z, self.n

        @pl.when(z < n - 1)
        def _():
            self.copy(c, z, 0).start()

        @pl.when(z > 0)
        def _():
            self.copy(c, z, 1).start()

    def forward(self, c):
        z, n = self.z, self.n
        for d in range(1, n):

            @pl.when(z - d >= 0)
            def _():
                self.copy(c, z - d, 0).wait_recv()

                @pl.when(z < n - 1)
                def _():
                    self.copy(c, z - d, 0).start()

            @pl.when(z + d <= n - 1)
            def _():
                self.copy(c, z + d, 1).wait_recv()

                @pl.when(z > 0)
                def _():
                    self.copy(c, z + d, 1).start()

    def finish(self, c):
        z, n = self.z, self.n
        for o in range(n):

            @pl.when((z >= o) & (z < n - 1))
            def _():
                self.copy(c, o, 0).wait_send()

            @pl.when((z <= o) & (z > 0))
            def _():
                self.copy(c, o, 1).wait_send()


class Scatter:
    def __init__(self, z, n, term, recv, send_sem, recv_sem):
        self.z, self.n, self.term, self.recv = z, n, term, recv
        self.send_sem, self.recv_sem = send_sem, recv_sem

    def copy(self, c, o, way):
        target = self.z + 1 if way == 0 else self.z - 1
        return line_copy(
            self.term.at[c, o],
            self.recv.at[way, c, o],
            self.send_sem.at[c, o],
            self.recv_sem.at[way, c, o],
            target,
        )

    def ends(self, c):
        z, n = self.z, self.n
        for k in range(n - 1):

            @pl.when(z == 0)
            def _():
                self.copy(c, n - 1 - k, 0).start()

            @pl.when(z == n - 1)
            def _():
                self.copy(c, k, 1).start()

    def add(self, c, o, way):
        self.copy(c, o, way).wait_recv()
        total = self.term[c, o].astype(jnp.float32) + self.recv[way, c, o].astype(jnp.float32)
        self.term[c, o] = total.astype(jnp.bfloat16)
        self.copy(c, o, way).start()

    def forward(self, c):
        z, n = self.z, self.n
        for k in range(n - 1):
            right, left = n - 1 - k, k

            @pl.when((z > 0) & (z < right))
            def _():
                self.add(c, right, 0)

            @pl.when((z < n - 1) & (z > left))
            def _():
                self.add(c, left, 1)

    def collect(self, c, total):
        z, n = self.z, self.n
        total[...] = self.term[c, z].astype(jnp.float32)

        @pl.when(z > 0)
        def _():
            self.copy(c, z, 0).wait_recv()
            total[...] += self.recv[0, c, z].astype(jnp.float32)

        @pl.when(z < n - 1)
        def _():
            self.copy(c, z, 1).wait_recv()
            total[...] += self.recv[1, c, z].astype(jnp.float32)

    def finish(self, c):
        z, n = self.z, self.n
        for o in range(n):

            @pl.when(z < o)
            def _():
                self.copy(c, o, 0).wait_send()

            @pl.when(z > o)
            def _():
                self.copy(c, o, 1).wait_send()


def tail_kernel(
    n,
    chunks,
    last,
    step_ref,
    mixed_ref,
    out_weight_ref,
    latent_ref,
    mods_ref,
    next_ref,
    fc_in_ref,
    fc_out_ref,
    new_ref,
    velocity_ref,
    gathered_ref,
    attn_term,
    attn_recv,
    mlp_in_all,
    mlp_term,
    mlp_recv,
    attn_sum,
    total,
    hidden_ref,
    as_send,
    as_recv,
    mg_send,
    mg_recv,
    ms_send,
    ms_recv,
    ag_send,
    ag_recv,
):
    z = lax.axis_index("tensor")
    tokens, width = latent_ref.shape
    rows = tokens // chunks
    tile = math.gcd(width, 768)
    attn_out = Scatter(z, n, attn_term, attn_recv, as_send, as_recv)
    mlp_gather = Gather(z, n, mlp_in_all, mg_send, mg_recv)
    mlp_out = Scatter(z, n, mlp_term, mlp_recv, ms_send, ms_recv)
    next_gather = None if last else Gather(z, n, gathered_ref, ag_send, ag_recv)

    greet_neighbours(z, n)
    for c in range(chunks):
        part = mixed_ref[c * n * rows : (c + 1) * n * rows, :]
        for t in range(0, width, tile):
            product = lax.dot_general(
                part,
                out_weight_ref[t : t + tile, :],
                (((1,), (1,)), ((), ())),
                preferred_element_type=jnp.float32,
            ).astype(jnp.bfloat16)
            attn_term[c, :, :, t : t + tile] = product.reshape(n, rows, tile)
        attn_out.ends(c)

    def after_attention(c):
        attn_out.forward(c)
        attn_out.collect(c, attn_sum.at[c])
        own = slice(c * rows, (c + 1) * rows)
        gated = mods_ref[2:3, :] * attn_sum[c]
        midway = latent_ref[own, :] + gated
        attn_sum[c] = gated
        mlp_in = layer_norm(midway) * (1.0 + mods_ref[4:5, :]) + mods_ref[3:4, :]
        mlp_in_all[c, z] = mlp_in.astype(jnp.bfloat16)
        mlp_gather.start(c)

    def feed_forward(c):
        mlp_gather.forward(c)
        tokens_in = mlp_in_all[c].reshape(n * rows, width)
        hidden = jax.nn.gelu(
            jnp.dot(tokens_in, fc_in_ref[...], preferred_element_type=jnp.float32),
            approximate=True,
        )
        hidden_ref[...] = hidden.astype(jnp.bfloat16)
        for t in range(0, width, tile):
            product = jnp.dot(
                hidden_ref[...], fc_out_ref[:, t : t + tile], preferred_element_type=jnp.float32
            ).astype(jnp.bfloat16)
            mlp_term[c, :, :, t : t + tile] = product.reshape(n, rows, tile)
        mlp_out.ends(c)

    def after_feed_forward(c):
        mlp_out.forward(c)
        mlp_out.collect(c, total)
        own = slice(c * rows, (c + 1) * rows)
        update = attn_sum[c] + mods_ref[5:6, :] * total[...]
        velocity_ref[own, :] = update.astype(jnp.bfloat16)
        fresh = latent_ref[own, :] + step_ref[0:1, 0:1] * update
        new_ref[own, :] = fresh.astype(new_ref.dtype)
        if not last:
            attn_in = layer_norm(fresh) * (1.0 + next_ref[1:2, :]) + next_ref[0:1, :]
            gathered_ref[c, z] = attn_in.astype(jnp.bfloat16)
            next_gather.start(c)

    stages = [after_attention, feed_forward, after_feed_forward]
    if not last:
        stages.append(lambda c: next_gather.forward(c))
    for tick in range(chunks + len(stages) - 1):
        for place, stage in enumerate(stages):
            if 0 <= tick - place < chunks:
                stage(tick - place)
    for c in range(chunks):
        attn_out.finish(c)
        mlp_gather.finish(c)
        mlp_out.finish(c)
        if not last:
            next_gather.finish(c)


def chunk_count(tokens):
    return max(1, min(2, tokens // 16))


def block_tail(n, last, step_size, mixed, out_weight, latent, mods, next_mods, fc_in, fc_out):
    tokens, width = latent.shape
    chunks = chunk_count(tokens)
    rows = tokens // chunks
    blocks = (chunks, n, rows, width)
    vmem = pl.BlockSpec(memory_space=pltpu.VMEM)
    gathered_shape = (8, 128) if last else blocks
    dma = pltpu.SemaphoreType.DMA
    return pl.pallas_call(
        functools.partial(tail_kernel, n, chunks, last),
        out_shape=(
            jax.ShapeDtypeStruct((tokens, width), jnp.bfloat16 if last else jnp.float32),
            jax.ShapeDtypeStruct((tokens, width), jnp.bfloat16),
            jax.ShapeDtypeStruct(gathered_shape, jnp.bfloat16),
        ),
        in_specs=[vmem] * 8,
        out_specs=(vmem, vmem, vmem),
        scratch_shapes=[
            pltpu.VMEM(blocks, jnp.bfloat16),
            pltpu.VMEM((2,) + blocks, jnp.bfloat16),
            pltpu.VMEM(blocks, jnp.bfloat16),
            pltpu.VMEM(blocks, jnp.bfloat16),
            pltpu.VMEM((2,) + blocks, jnp.bfloat16),
            pltpu.VMEM((chunks, rows, width), jnp.float32),
            pltpu.VMEM((rows, width), jnp.float32),
            pltpu.VMEM((n * rows, fc_in.shape[1]), jnp.bfloat16),
            dma((chunks, n)),
            dma((2, chunks, n)),
            dma((2, chunks, n)),
            dma((chunks, n)),
            dma((chunks, n)),
            dma((2, chunks, n)),
            dma((2, chunks, n)),
            dma((chunks, n)),
        ],
        compiler_params=pltpu.CompilerParams(
            collective_id=1 if last else 0,
            has_side_effects=True,
            vmem_limit_bytes=48 * 1024 * 1024,
        ),
        cost_estimate=pl.CostEstimate(
            flops=4 * n * tokens * width * fc_in.shape[1],
            bytes_accessed=4 * width * fc_in.shape[1],
            transcendentals=n * tokens * fc_in.shape[1],
        ),
    )(step_size, mixed, out_weight, latent, mods, next_mods, fc_in, fc_out)


def mesh_copy(src, dst, send_sem, recv_sem, axis, target):
    return pltpu.make_async_remote_copy(
        src_ref=src,
        dst_ref=dst,
        send_sem=send_sem,
        recv_sem=recv_sem,
        device_id={axis: target},
        device_id_type=pl.DeviceIdType.MESH,
    )


def head_kernel(
    n,
    owners,
    chunks,
    mod_ref,
    video_ref,
    delta_ref,
    modulation_ref,
    gathered_ref,
    pieces_ref,
    mod_all,
    own_sem,
    mod_send,
    mod_recv,
    line_send,
    line_recv,
    chip_send,
    chip_recv,
    twin_send,
    twin_recv,
    ag_send,
    ag_recv,
):
    z = lax.axis_index("tensor")
    f = lax.axis_index("fsdp")
    chip = f // 2
    core = f - 2 * chip
    twin = 2 * chip + 1 - core
    chips = owners // 2
    tokens, width = video_ref.shape
    rows = tokens // chunks
    head_width = pieces_ref.shape[3]
    barrier = pltpu.get_barrier_semaphore()

    def greet(axis, target):
        pl.semaphore_signal(
            barrier, inc=1, device_id={axis: target}, device_id_type=pl.DeviceIdType.MESH
        )

    for d in range(1, n):
        greet("tensor", lax.rem(z + d, n))
    greet("fsdp", twin)
    for d in range(1, chips):
        greet("fsdp", 2 * lax.rem(chip + d, chips) + core)
    pl.semaphore_wait(barrier, n - 1 + chips)

    def mod_copy(owner, d):
        return mesh_copy(
            mod_ref,
            mod_all.at[owner],
            mod_send.at[d],
            mod_recv.at[owner],
            "tensor",
            lax.rem(z + d, n),
        )

    def columns(target):
        return delta_ref.at[:, :, pl.ds(pl.multiple_of(target * head_width, head_width), head_width)]

    def line_piece(owner, d):
        target = lax.rem(z + d, n)
        return mesh_copy(
            columns(target),
            pieces_ref.at[f * n + owner],
            line_send.at[d],
            line_recv.at[owner],
            "tensor",
            target,
        )

    def chip_piece(source, t, d):
        piece = pieces_ref.at[source * n + t]
        return mesh_copy(
            piece,
            piece,
            chip_send.at[d, t],
            chip_recv.at[source, t],
            "fsdp",
            2 * lax.rem(chip + d, chips) + core,
        )

    def twin_piece(source, t):
        piece = pieces_ref.at[source * n + t]
        return mesh_copy(
            piece, piece, twin_send.at[source, t], twin_recv.at[source, t], "fsdp", twin
        )

    def spread(t):
        for d in range(1, chips):
            chip_piece(f, t, d).start()
        twin_piece(f, t).start()

    for d in range(1, n):
        mod_copy(z, d).start()
    own = pltpu.make_async_copy(columns(z), pieces_ref.at[f * n + z], own_sem)
    own.start()
    for d in range(1, n):
        line_piece(z, d).start()
    mod_all[z] = mod_ref[...]
    own.wait()
    spread(z)
    for d in range(1, n):
        mod_copy(lax.rem(z + d, n), d).wait_recv()
    share = mod_ref.shape[1]
    for t in range(n):
        modulation_ref[:, t * share : (t + 1) * share] = mod_all[t]

    gather = Gather(z, n, gathered_ref, ag_send, ag_recv)
    for c in range(chunks):
        values = video_ref[c * rows : (c + 1) * rows, :].astype(jnp.float32)
        attn_in = layer_norm(values) * (1.0 + modulation_ref[1:2, :]) + modulation_ref[0:1, :]
        gathered_ref[c, z] = attn_in.astype(jnp.bfloat16)
        gather.start(c)

    for d in range(1, n):
        owner = lax.rem(z + d, n)
        line_piece(owner, d).wait_recv()
        spread(owner)

    def arrive(k):
        for d in range(1, chips):
            source = 2 * lax.rem(chip + d, chips) + core
            t = lax.rem(z + k, n)
            chip_piece(source, t, d).wait_recv()
            twin_piece(source, t).start()

    steps = n // chunks
    for c in range(chunks):
        gather.forward(c)
        for k in range(c * steps, n if c == chunks - 1 else (c + 1) * steps):
            arrive(k)
    for c in range(chunks):
        gather.finish(c)
    for j in range(chips):
        source = 2 * j + 1 - core
        for t in range(n):
            twin_piece(source, t).wait_recv()
            twin_piece(2 * j + core, t).wait_send()
    for d in range(1, n):
        mod_copy(z, d).wait_send()
        line_piece(z, d).wait_send()
    for d in range(1, chips):
        for t in range(n):
            chip_piece(f, t, d).wait_send()


def block_head(n, owners, mod_part, video, delta_values):
    tokens, width = video.shape
    mats, piece_rows, columns = delta_values.shape
    chunks = chunk_count(tokens)
    vmem = pl.BlockSpec(memory_space=pltpu.VMEM)
    dma = pltpu.SemaphoreType.DMA
    return pl.pallas_call(
        functools.partial(head_kernel, n, owners, chunks),
        out_shape=(
            jax.ShapeDtypeStruct((mod_part.shape[0], width), jnp.float32),
            jax.ShapeDtypeStruct((chunks, n, tokens // chunks, width), jnp.bfloat16),
            jax.ShapeDtypeStruct((owners * n, mats, piece_rows, columns // n), jnp.bfloat16),
        ),
        in_specs=[vmem] * 3,
        out_specs=(vmem, vmem, vmem),
        scratch_shapes=[
            pltpu.VMEM((n,) + mod_part.shape, jnp.float32),
            dma(()),
            dma((n,)),
            dma((n,)),
            dma((n,)),
            dma((n,)),
            dma((max(owners // 2, 1), n)),
            dma((owners, n)),
            dma((owners, n)),
            dma((owners, n)),
            dma((2, chunks, n)),
            dma((chunks, n)),
        ],
        compiler_params=pltpu.CompilerParams(
            collective_id=2,
            has_side_effects=True,
            vmem_limit_bytes=40 * 1024 * 1024,
        ),
        cost_estimate=pl.CostEstimate(
            flops=10 * tokens * width, bytes_accessed=8 * tokens * n * width, transcendentals=0
        ),
    )(mod_part, video, delta_values)


def shards(
    video,
    timesteps,
    text_keys,
    text_values,
    text_lengths,
    base_weights,
    delta_values,
    delta_scales,
    q_gain,
    k_gain,
    mod_weight,
    fc_in,
    fc_out,
):
    head_dim = q_gain.shape[0]
    head_width = base_weights.shape[2]
    heads_here = head_width // head_dim
    text_count = text_keys.shape[1]
    column_index = lax.axis_index("tensor")
    embedding = jax.nn.silu(time_embed(timesteps[0, :STEPS], mod_weight.shape[0])).astype(
        jnp.bfloat16
    )
    mod_part = jnp.einsum("sf,fkd->skd", embedding, mod_weight, preferred_element_type=jnp.float32)
    n = lax.axis_size("tensor")
    owners = lax.axis_size("fsdp")
    width = video.shape[2]
    modulation, piece, delta_pieces = block_head(
        n, owners, mod_part.reshape(-1, mod_part.shape[2]), video[0], delta_values
    )
    modulation = modulation.reshape(STEPS, -1, width)
    piece = piece.reshape(-1, width)
    own_scales = lax.dynamic_slice_in_dim(delta_scales, column_index * heads_here, heads_here, 2)
    row_scales = jnp.repeat(own_scales, head_dim, axis=1)
    dequantize_piece = delta_pieces.swapaxes(0, 1).reshape(base_weights.shape)
    scale_full = jnp.repeat(row_scales, head_dim, axis=2)
    weights = (
        base_weights.astype(jnp.float32) + dequantize_piece.astype(jnp.float32) * scale_full
    ).astype(jnp.bfloat16)
    qkv_weights = weights[:3]
    out_weight = weights[3]
    latent = video[0].astype(jnp.float32)
    text_valid = jnp.arange(text_count) < text_lengths[0]
    text_k = text_keys[0]
    text_v = text_values[0]
    velocities = []
    for step in range(STEPS):
        mods = modulation[step]
        count = piece.shape[0]
        joined = jnp.einsum("rd,kdc->rkc", piece, qkv_weights, preferred_element_type=jnp.float32)
        query = rms_scale(joined[:, 0].reshape(count, heads_here, head_dim), q_gain).reshape(
            count, head_width
        )
        key_part = rms_scale(joined[:, 1].reshape(count, heads_here, head_dim), k_gain).reshape(
            count, head_width
        )
        projected = jnp.stack([query, key_part, joined[:, 2]], axis=1).astype(jnp.bfloat16)
        video_count = projected.shape[0]
        query = projected[:, 0].reshape(video_count, heads_here, head_dim)
        all_keys = jnp.concatenate([projected[:, 1], text_k], axis=0).reshape(
            -1, heads_here, head_dim
        )
        all_values = jnp.concatenate([projected[:, 2], text_v], axis=0).reshape(
            -1, heads_here, head_dim
        )
        key_valid = jnp.concatenate([jnp.ones((video_count,), dtype=bool), text_valid])
        scores = jnp.einsum(
            "qhd,khd->hqk", query, all_keys, preferred_element_type=jnp.float32
        ) / math.sqrt(head_dim)
        scores = jnp.where(key_valid[None, None, :], scores, -jnp.inf)
        soft = jax.nn.softmax(scores, axis=-1).astype(jnp.bfloat16)
        mixed = jnp.einsum(
            "hqk,khd->qhd", soft, all_values, preferred_element_type=jnp.float32
        ).astype(jnp.bfloat16)
        mixed = mixed.reshape(video_count, head_width)
        step_size = (timesteps[0, step + 1] - timesteps[0, step]).astype(jnp.float32) / 1000.0
        last = step == STEPS - 1
        latent, velocity, gathered = block_tail(
            n,
            last,
            step_size.reshape(1, 1),
            mixed,
            out_weight,
            latent,
            mods,
            mods if last else modulation[step + 1],
            fc_in,
            fc_out,
        )
        velocities.append(velocity)
        if not last:
            piece = gathered.reshape(-1, width)
    return (latent[None], jnp.stack(velocities)[None])


def solution(mesh):
    in_specs = (
        P(("groups", "fsdp"), "tensor", None),
        P(("groups", "fsdp"), None),
        P(("groups", "fsdp"), None, "tensor"),
        P(("groups", "fsdp"), None, "tensor"),
        P(("groups", "fsdp")),
        P(None, None, "tensor"),
        P(None, ("fsdp", "tensor"), None),
        P(),
        P(),
        P(),
        P(None, None, "tensor"),
        P(None, "tensor"),
        P("tensor", None),
    )
    out_specs = (P(("groups", "fsdp"), "tensor", None), P(("groups", "fsdp"), None, "tensor", None))
    return jax.shard_map(shards, mesh=mesh, in_specs=in_specs, out_specs=out_specs, check_vma=False)
```

```python
import functools
import math

import jax
import jax.numpy as jnp
from jax import lax
from jax.experimental import pallas as pl
from jax.experimental.pallas import tpu as pltpu
from jax.sharding import PartitionSpec as P

STEPS = 2


def layer_norm(values):
    center = values - jnp.mean(values, axis=-1, keepdims=True)
    spread = jnp.mean(center * center, axis=-1, keepdims=True)
    return center * lax.rsqrt(spread + 1e-06)


def rms_scale(values, gain):
    power = jnp.mean(values * values, axis=-1, keepdims=True)
    return values * lax.rsqrt(power + 1e-06) * gain


def time_embed(times, freq_count):
    half_count = freq_count // 2
    ladder = jnp.exp(-math.log(10000.0) * jnp.arange(half_count, dtype=jnp.float32) / half_count)
    angles = times.astype(jnp.float32)[:, None] * ladder[None, :]
    return jnp.concatenate([jnp.cos(angles), jnp.sin(angles)], axis=1)


def line_copy(src, dst, send_sem, recv_sem, target):
    return pltpu.make_async_remote_copy(
        src_ref=src,
        dst_ref=dst,
        send_sem=send_sem,
        recv_sem=recv_sem,
        device_id={"tensor": target},
        device_id_type=pl.DeviceIdType.MESH,
    )


def greet_neighbours(z, n):
    barrier = pltpu.get_barrier_semaphore()

    @pl.when(z > 0)
    def _():
        pl.semaphore_signal(
            barrier, inc=1, device_id={"tensor": z - 1}, device_id_type=pl.DeviceIdType.MESH
        )

    @pl.when(z < n - 1)
    def _():
        pl.semaphore_signal(
            barrier, inc=1, device_id={"tensor": z + 1}, device_id_type=pl.DeviceIdType.MESH
        )


def await_neighbours(z, n):
    pl.semaphore_wait(
        pltpu.get_barrier_semaphore(), jnp.where(z > 0, 1, 0) + jnp.where(z < n - 1, 1, 0)
    )


class Gather:
    def __init__(self, z, n, buf, send_sem, recv_sem):
        self.z, self.n, self.buf, self.send_sem, self.recv_sem = z, n, buf, send_sem, recv_sem

    def copy(self, c, owner, way):
        block = self.buf.at[c, owner]
        target = self.z + 1 if way == 0 else self.z - 1
        return line_copy(
            block, block, self.send_sem.at[way, c, owner], self.recv_sem.at[c, owner], target
        )

    def start(self, c):
        z, n = self.z, self.n

        @pl.when(z < n - 1)
        def _():
            self.copy(c, z, 0).start()

        @pl.when(z > 0)
        def _():
            self.copy(c, z, 1).start()

    def forward(self, c, k):
        z, n = self.z, self.n
        d = k + 1

        @pl.when(z - d >= 0)
        def _():
            self.copy(c, z - d, 0).wait_recv()

            @pl.when(z < n - 1)
            def _():
                self.copy(c, z - d, 0).start()

        @pl.when(z + d <= n - 1)
        def _():
            self.copy(c, z + d, 1).wait_recv()

            @pl.when(z > 0)
            def _():
                self.copy(c, z + d, 1).start()

    def finish(self, c):
        z, n = self.z, self.n
        for o in range(n):

            @pl.when((z >= o) & (z < n - 1))
            def _():
                self.copy(c, o, 0).wait_send()

            @pl.when((z <= o) & (z > 0))
            def _():
                self.copy(c, o, 1).wait_send()


class Scatter:
    def __init__(self, z, n, term, recv, send_sem, recv_sem):
        self.z, self.n, self.term, self.recv = z, n, term, recv
        self.send_sem, self.recv_sem = send_sem, recv_sem

    def copy(self, c, o, way):
        target = self.z + 1 if way == 0 else self.z - 1
        return line_copy(
            self.term.at[c, o],
            self.recv.at[way, c, o],
            self.send_sem.at[c, o],
            self.recv_sem.at[way, c, o],
            target,
        )

    def ends(self, c):
        z, n = self.z, self.n
        for k in range(n - 1):

            @pl.when(z == 0)
            def _():
                self.copy(c, n - 1 - k, 0).start()

            @pl.when(z == n - 1)
            def _():
                self.copy(c, k, 1).start()

    def add(self, c, o, way):
        self.copy(c, o, way).wait_recv()
        total = self.term[c, o].astype(jnp.float32) + self.recv[way, c, o].astype(jnp.float32)
        self.term[c, o] = total.astype(jnp.bfloat16)
        self.copy(c, o, way).start()

    def forward(self, c, k):
        z, n = self.z, self.n
        turn = k + 1
        if turn == n - 1:
            return

        @pl.when((z > 0) & (z <= turn))
        def _():
            self.add(c, z + n - 1 - turn, 0)

        @pl.when((z < n - 1) & (z >= n - 1 - turn))
        def _():
            self.add(c, z - (n - 1 - turn), 1)

    def collect(self, c, total):
        z, n = self.z, self.n
        total[...] = self.term[c, z].astype(jnp.float32)

        @pl.when(z > 0)
        def _():
            self.copy(c, z, 0).wait_recv()
            total[...] += self.recv[0, c, z].astype(jnp.float32)

        @pl.when(z < n - 1)
        def _():
            self.copy(c, z, 1).wait_recv()
            total[...] += self.recv[1, c, z].astype(jnp.float32)

    def finish(self, c):
        z, n = self.z, self.n
        for o in range(n):

            @pl.when(z < o)
            def _():
                self.copy(c, o, 0).wait_send()

            @pl.when(z > o)
            def _():
                self.copy(c, o, 1).wait_send()


def tail_kernel(
    n,
    chunks,
    last,
    step_ref,
    mixed_ref,
    out_weight_ref,
    latent_ref,
    mods_ref,
    next_ref,
    fc_in_hbm,
    fc_out_hbm,
    new_ref,
    velocity_ref,
    gathered_ref,
    attn_term,
    attn_recv,
    mlp_in_all,
    mlp_term,
    mlp_recv,
    attn_sum,
    total,
    hidden_ref,
    fc_in_ref,
    fc_out_ref,
    load_sem,
    as_send,
    as_recv,
    mg_send,
    mg_recv,
    ms_send,
    ms_recv,
    ag_send,
    ag_recv,
):
    z = lax.axis_index("tensor")
    tokens, width = latent_ref.shape
    rows = tokens // chunks
    tile = math.gcd(width, 768)
    attn_out = Scatter(z, n, attn_term, attn_recv, as_send, as_recv)
    mlp_gather = Gather(z, n, mlp_in_all, mg_send, mg_recv)
    mlp_out = Scatter(z, n, mlp_term, mlp_recv, ms_send, ms_recv)
    next_gather = None if last else Gather(z, n, gathered_ref, ag_send, ag_recv)

    greet_neighbours(z, n)
    loads = [
        pltpu.make_async_copy(fc_in_hbm, fc_in_ref, load_sem.at[0]),
        pltpu.make_async_copy(fc_out_hbm, fc_out_ref, load_sem.at[1]),
    ]
    for load in loads:
        load.start()
    for c in range(chunks):
        part = mixed_ref[c * n * rows : (c + 1) * n * rows, :]
        for t in range(0, width, tile):
            product = lax.dot_general(
                part,
                out_weight_ref[t : t + tile, :],
                (((1,), (1,)), ((), ())),
                preferred_element_type=jnp.float32,
            ).astype(jnp.bfloat16)
            attn_term[c, :, :, t : t + tile] = product.reshape(n, rows, tile)
    await_neighbours(z, n)
    for c in range(chunks):
        attn_out.ends(c)

    def after_attention(c):
        attn_out.collect(c, attn_sum.at[c])
        own = slice(c * rows, (c + 1) * rows)
        gated = mods_ref[2:3, :] * attn_sum[c]
        midway = latent_ref[own, :] + gated
        attn_sum[c] = gated
        mlp_in = layer_norm(midway) * (1.0 + mods_ref[4:5, :]) + mods_ref[3:4, :]
        mlp_in_all[c, z] = mlp_in.astype(jnp.bfloat16)
        mlp_gather.start(c)

    def feed_forward(c):
        if c == 0:
            for load in loads:
                load.wait()
        tokens_in = mlp_in_all[c].reshape(n * rows, width)
        hidden = jax.nn.gelu(
            jnp.dot(tokens_in, fc_in_ref[...], preferred_element_type=jnp.float32),
            approximate=True,
        )
        hidden_ref[...] = hidden.astype(jnp.bfloat16)
        for t in range(0, width, tile):
            product = jnp.dot(
                hidden_ref[...], fc_out_ref[:, t : t + tile], preferred_element_type=jnp.float32
            ).astype(jnp.bfloat16)
            mlp_term[c, :, :, t : t + tile] = product.reshape(n, rows, tile)
        mlp_out.ends(c)

    def after_feed_forward(c):
        mlp_out.collect(c, total)
        own = slice(c * rows, (c + 1) * rows)
        update = attn_sum[c] + mods_ref[5:6, :] * total[...]
        velocity_ref[own, :] = update.astype(jnp.bfloat16)
        fresh = latent_ref[own, :] + step_ref[0:1, 0:1] * update
        new_ref[own, :] = fresh.astype(new_ref.dtype)
        if not last:
            attn_in = layer_norm(fresh) * (1.0 + next_ref[1:2, :]) + next_ref[0:1, :]
            gathered_ref[c, z] = attn_in.astype(jnp.bfloat16)
            next_gather.start(c)

    stages = [
        (attn_out.forward, after_attention),
        (mlp_gather.forward, feed_forward),
        (mlp_out.forward, after_feed_forward),
    ]
    if not last:
        stages.append((next_gather.forward, None))
    for tick in range(chunks + len(stages) - 1):
        active = [
            (tick - place, stage)
            for place, stage in enumerate(stages)
            if 0 <= tick - place < chunks
        ]
        for k in range(n - 1):
            for c, stage in active:
                stage[0](c, k)
        for c, stage in active:
            if stage[1] is not None:
                stage[1](c)
    for c in range(chunks):
        attn_out.finish(c)
        mlp_gather.finish(c)
        mlp_out.finish(c)
        if not last:
            next_gather.finish(c)


def chunk_count(tokens):
    return max(1, min(2, tokens // 16))


def block_tail(n, last, step_size, mixed, out_weight, latent, mods, next_mods, fc_in, fc_out):
    tokens, width = latent.shape
    chunks = chunk_count(tokens)
    rows = tokens // chunks
    blocks = (chunks, n, rows, width)
    vmem = pl.BlockSpec(memory_space=pltpu.VMEM)
    gathered_shape = (8, 128) if last else blocks
    dma = pltpu.SemaphoreType.DMA
    return pl.pallas_call(
        functools.partial(tail_kernel, n, chunks, last),
        out_shape=(
            jax.ShapeDtypeStruct((tokens, width), jnp.bfloat16 if last else jnp.float32),
            jax.ShapeDtypeStruct((tokens, width), jnp.bfloat16),
            jax.ShapeDtypeStruct(gathered_shape, jnp.bfloat16),
        ),
        in_specs=[vmem] * 6 + [pl.BlockSpec(memory_space=pl.ANY)] * 2,
        out_specs=(vmem, vmem, vmem),
        scratch_shapes=[
            pltpu.VMEM(blocks, jnp.bfloat16),
            pltpu.VMEM((2,) + blocks, jnp.bfloat16),
            pltpu.VMEM(blocks, jnp.bfloat16),
            pltpu.VMEM(blocks, jnp.bfloat16),
            pltpu.VMEM((2,) + blocks, jnp.bfloat16),
            pltpu.VMEM((chunks, rows, width), jnp.float32),
            pltpu.VMEM((rows, width), jnp.float32),
            pltpu.VMEM((n * rows, fc_in.shape[1]), jnp.bfloat16),
            pltpu.VMEM(fc_in.shape, jnp.bfloat16),
            pltpu.VMEM(fc_out.shape, jnp.bfloat16),
            dma((2,)),
            dma((chunks, n)),
            dma((2, chunks, n)),
            dma((2, chunks, n)),
            dma((chunks, n)),
            dma((chunks, n)),
            dma((2, chunks, n)),
            dma((2, chunks, n)),
            dma((chunks, n)),
        ],
        compiler_params=pltpu.CompilerParams(
            collective_id=1 if last else 0,
            has_side_effects=True,
            vmem_limit_bytes=48 * 1024 * 1024,
        ),
        cost_estimate=pl.CostEstimate(
            flops=4 * n * tokens * width * fc_in.shape[1],
            bytes_accessed=4 * width * fc_in.shape[1],
            transcendentals=n * tokens * fc_in.shape[1],
        ),
    )(step_size, mixed, out_weight, latent, mods, next_mods, fc_in, fc_out)


def mesh_copy(src, dst, send_sem, recv_sem, axis, target):
    return pltpu.make_async_remote_copy(
        src_ref=src,
        dst_ref=dst,
        send_sem=send_sem,
        recv_sem=recv_sem,
        device_id={axis: target},
        device_id_type=pl.DeviceIdType.MESH,
    )


def head_kernel(
    n,
    owners,
    chunks,
    mod_ref,
    video_ref,
    delta_ref,
    modulation_ref,
    gathered_ref,
    pieces_ref,
    mod_all,
    own_sem,
    mod_send,
    mod_recv,
    line_send,
    line_recv,
    chip_send,
    chip_recv,
    twin_send,
    twin_recv,
    ag_send,
    ag_recv,
):
    z = lax.axis_index("tensor")
    f = lax.axis_index("fsdp")
    chip = f // 2
    core = f - 2 * chip
    twin = 2 * chip + 1 - core
    chips = owners // 2
    tokens, width = video_ref.shape
    rows = tokens // chunks
    head_width = pieces_ref.shape[3]
    barrier = pltpu.get_barrier_semaphore()

    def greet(axis, target):
        pl.semaphore_signal(
            barrier, inc=1, device_id={axis: target}, device_id_type=pl.DeviceIdType.MESH
        )

    for d in range(1, n):
        greet("tensor", lax.rem(z + d, n))
    greet("fsdp", twin)
    for d in range(1, chips):
        greet("fsdp", 2 * lax.rem(chip + d, chips) + core)
    pl.semaphore_wait(barrier, n - 1 + chips)

    def mod_copy(owner, d):
        return mesh_copy(
            mod_ref,
            mod_all.at[owner],
            mod_send.at[d],
            mod_recv.at[owner],
            "tensor",
            lax.rem(z + d, n),
        )

    def columns(target):
        return delta_ref.at[:, :, pl.ds(pl.multiple_of(target * head_width, head_width), head_width)]

    def line_piece(owner, d):
        target = lax.rem(z + d, n)
        return mesh_copy(
            columns(target),
            pieces_ref.at[f * n + owner],
            line_send.at[d],
            line_recv.at[owner],
            "tensor",
            target,
        )

    def chip_piece(source, t, d):
        piece = pieces_ref.at[source * n + t]
        return mesh_copy(
            piece,
            piece,
            chip_send.at[d, t],
            chip_recv.at[source, t],
            "fsdp",
            2 * lax.rem(chip + d, chips) + core,
        )

    def twin_piece(source, t):
        piece = pieces_ref.at[source * n + t]
        return mesh_copy(
            piece, piece, twin_send.at[source, t], twin_recv.at[source, t], "fsdp", twin
        )

    def spread(t):
        for d in range(1, chips):
            chip_piece(f, t, d).start()
        twin_piece(f, t).start()

    for d in range(1, n):
        mod_copy(z, d).start()
    own = pltpu.make_async_copy(columns(z), pieces_ref.at[f * n + z], own_sem)
    own.start()
    for d in range(1, n):
        line_piece(z, d).start()
    mod_all[z] = mod_ref[...]
    own.wait()
    spread(z)
    for d in range(1, n):
        mod_copy(lax.rem(z + d, n), d).wait_recv()
    share = mod_ref.shape[1]
    for t in range(n):
        modulation_ref[:, t * share : (t + 1) * share] = mod_all[t]

    gather = Gather(z, n, gathered_ref, ag_send, ag_recv)
    for c in range(chunks):
        values = video_ref[c * rows : (c + 1) * rows, :].astype(jnp.float32)
        attn_in = layer_norm(values) * (1.0 + modulation_ref[1:2, :]) + modulation_ref[0:1, :]
        gathered_ref[c, z] = attn_in.astype(jnp.bfloat16)
        gather.start(c)

    for d in range(1, n):
        owner = lax.rem(z + d, n)
        line_piece(owner, d).wait_recv()
        spread(owner)

    def arrive(k):
        for d in range(1, chips):
            source = 2 * lax.rem(chip + d, chips) + core
            t = lax.rem(z + k, n)
            chip_piece(source, t, d).wait_recv()
            twin_piece(source, t).start()

    steps = n // chunks
    for c in range(chunks):
        for k in range(n - 1):
            gather.forward(c, k)
        for k in range(c * steps, n if c == chunks - 1 else (c + 1) * steps):
            arrive(k)
    for c in range(chunks):
        gather.finish(c)
    for j in range(chips):
        source = 2 * j + 1 - core
        for t in range(n):
            twin_piece(source, t).wait_recv()
            twin_piece(2 * j + core, t).wait_send()
    for d in range(1, n):
        mod_copy(z, d).wait_send()
        line_piece(z, d).wait_send()
    for d in range(1, chips):
        for t in range(n):
            chip_piece(f, t, d).wait_send()


def block_head(n, owners, mod_part, video, delta_values):
    tokens, width = video.shape
    mats, piece_rows, columns = delta_values.shape
    chunks = chunk_count(tokens)
    vmem = pl.BlockSpec(memory_space=pltpu.VMEM)
    dma = pltpu.SemaphoreType.DMA
    return pl.pallas_call(
        functools.partial(head_kernel, n, owners, chunks),
        out_shape=(
            jax.ShapeDtypeStruct((mod_part.shape[0], width), jnp.float32),
            jax.ShapeDtypeStruct((chunks, n, tokens // chunks, width), jnp.bfloat16),
            jax.ShapeDtypeStruct((owners * n, mats, piece_rows, columns // n), jnp.bfloat16),
        ),
        in_specs=[vmem] * 3,
        out_specs=(vmem, vmem, vmem),
        scratch_shapes=[
            pltpu.VMEM((n,) + mod_part.shape, jnp.float32),
            dma(()),
            dma((n,)),
            dma((n,)),
            dma((n,)),
            dma((n,)),
            dma((max(owners // 2, 1), n)),
            dma((owners, n)),
            dma((owners, n)),
            dma((owners, n)),
            dma((2, chunks, n)),
            dma((chunks, n)),
        ],
        compiler_params=pltpu.CompilerParams(
            collective_id=2,
            has_side_effects=True,
            vmem_limit_bytes=40 * 1024 * 1024,
        ),
        cost_estimate=pl.CostEstimate(
            flops=10 * tokens * width, bytes_accessed=8 * tokens * n * width, transcendentals=0
        ),
    )(mod_part, video, delta_values)


def shards(
    video,
    timesteps,
    text_keys,
    text_values,
    text_lengths,
    base_weights,
    delta_values,
    delta_scales,
    q_gain,
    k_gain,
    mod_weight,
    fc_in,
    fc_out,
):
    head_dim = q_gain.shape[0]
    head_width = base_weights.shape[2]
    heads_here = head_width // head_dim
    text_count = text_keys.shape[1]
    column_index = lax.axis_index("tensor")
    embedding = jax.nn.silu(time_embed(timesteps[0, :STEPS], mod_weight.shape[0])).astype(
        jnp.bfloat16
    )
    mod_part = jnp.einsum("sf,fkd->skd", embedding, mod_weight, preferred_element_type=jnp.float32)
    n = lax.axis_size("tensor")
    owners = lax.axis_size("fsdp")
    width = video.shape[2]
    modulation, piece, delta_pieces = block_head(
        n, owners, mod_part.reshape(-1, mod_part.shape[2]), video[0], delta_values
    )
    modulation = modulation.reshape(STEPS, -1, width)
    piece = piece.reshape(-1, width)
    own_scales = lax.dynamic_slice_in_dim(delta_scales, column_index * heads_here, heads_here, 2)
    row_scales = jnp.repeat(own_scales, head_dim, axis=1)
    dequantize_piece = delta_pieces.swapaxes(0, 1).reshape(base_weights.shape)
    scale_full = jnp.repeat(row_scales, head_dim, axis=2)
    weights = (
        base_weights.astype(jnp.float32) + dequantize_piece.astype(jnp.float32) * scale_full
    ).astype(jnp.bfloat16)
    qkv_weights = weights[:3]
    out_weight = weights[3]
    latent = video[0].astype(jnp.float32)
    text_valid = jnp.arange(text_count) < text_lengths[0]
    text_k = text_keys[0]
    text_v = text_values[0]
    velocities = []
    for step in range(STEPS):
        mods = modulation[step]
        count = piece.shape[0]
        joined = jnp.einsum("rd,kdc->rkc", piece, qkv_weights, preferred_element_type=jnp.float32)
        query = rms_scale(joined[:, 0].reshape(count, heads_here, head_dim), q_gain).reshape(
            count, head_width
        )
        key_part = rms_scale(joined[:, 1].reshape(count, heads_here, head_dim), k_gain).reshape(
            count, head_width
        )
        projected = jnp.stack([query, key_part, joined[:, 2]], axis=1).astype(jnp.bfloat16)
        video_count = projected.shape[0]
        query = projected[:, 0].reshape(video_count, heads_here, head_dim)
        all_keys = jnp.concatenate([projected[:, 1], text_k], axis=0).reshape(
            -1, heads_here, head_dim
        )
        all_values = jnp.concatenate([projected[:, 2], text_v], axis=0).reshape(
            -1, heads_here, head_dim
        )
        key_valid = jnp.concatenate([jnp.ones((video_count,), dtype=bool), text_valid])
        scores = jnp.einsum(
            "qhd,khd->hqk", query, all_keys, preferred_element_type=jnp.float32
        ) / math.sqrt(head_dim)
        scores = jnp.where(key_valid[None, None, :], scores, -jnp.inf)
        soft = jax.nn.softmax(scores, axis=-1).astype(jnp.bfloat16)
        mixed = jnp.einsum(
            "hqk,khd->qhd", soft, all_values, preferred_element_type=jnp.float32
        ).astype(jnp.bfloat16)
        mixed = mixed.reshape(video_count, head_width)
        step_size = (timesteps[0, step + 1] - timesteps[0, step]).astype(jnp.float32) / 1000.0
        last = step == STEPS - 1
        latent, velocity, gathered = block_tail(
            n,
            last,
            step_size.reshape(1, 1),
            mixed,
            out_weight,
            latent,
            mods,
            mods if last else modulation[step + 1],
            fc_in,
            fc_out,
        )
        velocities.append(velocity)
        if not last:
            piece = gathered.reshape(-1, width)
    return (latent[None], jnp.stack(velocities)[None])


def solution(mesh):
    in_specs = (
        P(("groups", "fsdp"), "tensor", None),
        P(("groups", "fsdp"), None),
        P(("groups", "fsdp"), None, "tensor"),
        P(("groups", "fsdp"), None, "tensor"),
        P(("groups", "fsdp")),
        P(None, None, "tensor"),
        P(None, ("fsdp", "tensor"), None),
        P(),
        P(),
        P(),
        P(None, None, "tensor"),
        P(None, "tensor"),
        P("tensor", None),
    )
    out_specs = (P(("groups", "fsdp"), "tensor", None), P(("groups", "fsdp"), None, "tensor", None))
    return jax.shard_map(shards, mesh=mesh, in_specs=in_specs, out_specs=out_specs, check_vma=False)
```
